256 devices in a mesh: section: 32 (over x_hi, z, core), tensor: 8 (over y, x_lo).
Axes of the slice: x: 4 (x_hi: 2, x_lo: 2; x = x_hi * 2 + x_lo), y: 4, z: 8, core: 2. Of those that a mesh axis runs over, the one named last changes fastest.
Arguments:
- x_in: bfloat16 [32, 256, 12288], P('section', None, 'tensor'), may hold values from -6 to 6
- grad_in: bfloat16 [32, 256, 12288], P('section', None, 'tensor'), may hold values from -8 to 8
- stash_near: bfloat16 [32, 256, 12288], P('section', None, 'tensor'), may hold values from -8 to 8
- parked_in: bfloat16 [32, 256, 12288], P('section', None, 'tensor'), may hold values from -6 to 6
- fresh: bfloat16 [256, 12288], P(None, 'tensor'), may hold values from -6 to 6
- loss_grad: bfloat16 [256, 12288], P(None, 'tensor'), may hold values from -6 to 6
- gain: float32 [32, 12288], P('section', 'tensor'), may hold values from 0.1 to 1.9
- qgain: float32 [32, 12288], P('section', 'tensor'), may hold values from 0.25 to 450, as said below
- lengths: int32 [65], replicated, may hold values from 64 to 256, as said below
Outputs:
- forward_out: bfloat16 [32, 256, 12288], P('section', None, 'tensor')
- backward_out: bfloat16 [32, 256, 12288], P('section', None, 'tensor')
- parked_out: bfloat16 [32, 256, 12288], P('section', None, 'tensor')
- gain_grad: float32 [32, 12288], P('section', 'tensor')
- qgain_grad: float32 [32, 12288], P('section', 'tensor')
The draws below stay inside these ranges and needn't reach their ends.
Inputs may be any that keep to these rules, and one draw needn't show every extreme that they name: `lengths`: every micro-batch keeps at least a quarter of its tokens; in every draw some micro-batch is full. `qgain`: positive query gains.
All inputs are finite; a program needn't handle non-finite values.
Results may differ from the reference program's by a relative error of at most 0.013.
The reference program's roundings to bfloat16 on the way count: a program that leaves them out, or rounds other values in their place, can miss the bound.
Values may be sent and summed in bfloat16 or wider, within the bound.
No kernel may reach another device: no remote copies, remote signals or barrier semaphores. Data moves between devices by JAX's collectives and lax.ppermute only.
A program may use at most 64 MiB of HBM per device.

```python
import math
import jax
import jax.numpy as jnp
from jax import lax

D = 12288
HD = 128
TOK = 256
SECTIONS = 32
MICRO = 65


def common_direction(key, top_ratio, level):
    key = jax.random.fold_in(key, 11)
    signs = jnp.where(jax.random.bernoulli(key, 0.5, (SECTIONS, D)), 1.0, -1.0).astype(jnp.float32)
    position = jnp.arange(D, dtype=jnp.float32) / float(max(D - 1, 1))
    return signs * level * jnp.exp(position * math.log(top_ratio))[None, :]


def draw_stash_near(key, part):
    direction = common_direction(key, 3.0, 0.6)
    key = jax.random.fold_in(key, 5)
    noise = jax.random.truncated_normal(key, -5.0, 5.0, (SECTIONS, TOK, D), jnp.float32)
    return (direction[:, None, :] + noise).astype(jnp.bfloat16)


def draw_grad_in(key, part):
    direction = common_direction(key, 3.0, 0.6)
    key = jax.random.fold_in(key, 6)
    noise = jax.random.truncated_normal(key, -5.0, 5.0, (SECTIONS, TOK, D), jnp.float32)
    return (0.8 * direction[:, None, :] + noise).astype(jnp.bfloat16)


def draw_qgain(key, part):
    key = jax.random.fold_in(key, 7)
    key_head, key_feat = jax.random.split(key)
    heads_n = D // HD
    factor = jnp.exp(jax.random.uniform(key_head, (SECTIONS, heads_n), jnp.float32, math.log(0.5), math.log(4.0)))
    spread = jax.random.uniform(key_feat, (SECTIONS, heads_n, HD), jnp.float32, 0.5, 1.5)
    return (factor[:, :, None] * spread).reshape(SECTIONS, D)


def draw_lengths(key, part):
    key = jax.random.fold_in(key, 3)
    key_vals, key_pick = jax.random.split(key)
    values = jax.random.randint(key_vals, (MICRO,), TOK // 4, TOK + 1, dtype=jnp.int32)
    picked = jax.random.randint(key_pick, (), 0, MICRO, dtype=jnp.int32)
    return values.at[picked].set(TOK)


def block_levels(rng, shape, cuts, smallest, high):
    def one(axis_at, shards_of):
        heights = jax.random.uniform(jax.random.fold_in(jax.random.fold_in(rng, 6), axis_at), (shards_of,), jnp.float32, smallest / len(cuts), high / len(cuts))
        return jnp.repeat(jnp.exp(heights), shape[axis_at] // shards_of).reshape((-1,) + (1,) * (len(shape) - axis_at - 1))

    level = one(*cuts[0])
    for cut in cuts[1:]:
        level = level * one(*cut)
    return level


def gaussian(rng, extent, scale, most, cuts=(), kind=jnp.bfloat16):
    loudness = block_levels(rng, extent, cuts, -0.22, 0.18) if cuts else 1.0
    drawn = jax.random.normal(rng, extent, jnp.float32) * scale * loudness
    return jnp.minimum(jnp.maximum(drawn, -most), most).astype(kind)


def setup_inputs(seed: int = 0) -> dict:
    seeds = jax.random.split(jax.random.key(seed), 10)
    x_in = gaussian(seeds[0], (SECTIONS, TOK, D), 1.0, 6.0, ((0, 32), (2, 8)))
    grad_in = draw_grad_in(jax.random.fold_in(seeds[9], 71), 0)
    stash_near = draw_stash_near(jax.random.fold_in(seeds[9], 71), 0)
    parked_in = gaussian(seeds[3], (SECTIONS, TOK, D), 1.0, 6.0, ((0, 32), (2, 8)))
    fresh = gaussian(seeds[4], (TOK, D), 1.0, 6.0, ((1, 8),))
    loss_grad = gaussian(seeds[5], (TOK, D), 1.0, 6.0, ((1, 8),))
    gain = jnp.clip(1.0 + 0.18 * jax.random.normal(seeds[6], (SECTIONS, D), jnp.float32), 0.1, 1.9)
    qgain = draw_qgain(jax.random.fold_in(seeds[9], 71), 0)
    lengths = draw_lengths(jax.random.fold_in(seeds[9], 71), 0)
    return dict(x_in=x_in, grad_in=grad_in, stash_near=stash_near, parked_in=parked_in, fresh=fresh, loss_grad=loss_grad, gain=gain, qgain=qgain, lengths=lengths)


epsilon = 1e-05

def attention_weights(query, hidden, length):
    rows_n = query.shape[0]
    scores = jnp.einsum('ihd,jhd->hij', query.astype(jnp.float32), hidden.astype(jnp.float32)) * (1.0 / HD)
    row_ids = lax.broadcasted_iota(jnp.int32, (rows_n, rows_n), 0)
    col_ids = lax.broadcasted_iota(jnp.int32, (rows_n, rows_n), 1)
    allowed = (col_ids <= row_ids) & (col_ids < length)
    return jax.nn.softmax(jnp.where(allowed[None], scores, -jnp.inf), axis=-1)

def norm_parts(inputs, gain_row):
    in_float = inputs.astype(jnp.float32)
    inv_rms = lax.rsqrt(lax.optimization_barrier(jnp.mean(in_float * in_float, axis=-1, keepdims=True)) + epsilon)
    unit_rows = in_float * inv_rms
    return (in_float, inv_rms, unit_rows, unit_rows * gain_row)

def forward_layer(inputs, gain_row, qgain_row, length):
    rows_n = inputs.shape[0]
    in_float, inv_rms, unit_rows, normed = norm_parts(inputs, gain_row)
    hidden = normed.astype(jnp.bfloat16).reshape(rows_n, -1, HD)
    query = (normed * qgain_row).astype(jnp.bfloat16).reshape(rows_n, -1, HD)
    attend = attention_weights(query, hidden, length).astype(jnp.bfloat16)
    mixed = jnp.einsum('hij,jhd->ihd', attend.astype(jnp.float32), hidden.astype(jnp.float32))
    return (in_float + mixed.reshape(rows_n, -1)).astype(jnp.bfloat16)

def backward_layer(inputs, out_grad, gain_row, qgain_row, length):
    rows_n = inputs.shape[0]
    in_float, inv_rms, unit_rows, normed = norm_parts(inputs, gain_row)
    hidden = normed.astype(jnp.bfloat16).reshape(rows_n, -1, HD)
    query = (normed * qgain_row).astype(jnp.bfloat16).reshape(rows_n, -1, HD)
    attend = attention_weights(query, hidden, length)
    attend_b = attend.astype(jnp.bfloat16).astype(jnp.float32)
    grad_heads = out_grad.astype(jnp.float32).reshape(rows_n, -1, HD)
    hidden_f = hidden.astype(jnp.float32)
    d_value = jnp.einsum('hij,ihd->jhd', attend_b, grad_heads)
    d_attend = jnp.einsum('ihd,jhd->hij', grad_heads, hidden_f)
    d_score = attend * (d_attend - lax.optimization_barrier(jnp.sum(d_attend * attend, axis=-1, keepdims=True))) * (1.0 / HD)
    d_score = d_score.astype(jnp.bfloat16).astype(jnp.float32)
    d_query = jnp.einsum('hij,jhd->ihd', d_score, hidden_f).reshape(rows_n, -1)
    d_key = jnp.einsum('hij,ihd->jhd', d_score, query.astype(jnp.float32))
    d_normed = d_query * qgain_row + (d_key + d_value).reshape(rows_n, -1)
    qgain_part = lax.optimization_barrier(jnp.sum(d_query * normed, axis=0))
    gain_part = lax.optimization_barrier(jnp.sum(d_normed * unit_rows, axis=0))
    d_unit = d_normed * gain_row
    project = lax.optimization_barrier(jnp.mean(d_unit * unit_rows, axis=-1, keepdims=True))
    d_input = out_grad.astype(jnp.float32) + inv_rms * (d_unit - unit_rows * project)
    return (d_input.astype(jnp.bfloat16), gain_part, qgain_part)

def one_slot(packed):
    fwd_input, stored, out_grad, gain_row, qgain_row, len_fwd, len_bwd = packed
    layer_out = forward_layer(fwd_input, gain_row, qgain_row, len_fwd)
    d_input, gain_part, qgain_part = backward_layer(stored, out_grad, gain_row, qgain_row, len_bwd)
    return (layer_out, d_input, gain_part, qgain_part)

def reference(x_in, grad_in, stash_near, parked_in, fresh, loss_grad, gain, qgain, lengths):
    section_count = x_in.shape[0]
    section_ids = jnp.arange(section_count, dtype=jnp.int32)
    first_out, first_grad, gain_one, qgain_one = lax.map(one_slot, (x_in, stash_near, grad_in, gain, qgain, lengths[2 * section_count - 1 - section_ids], lengths[section_ids]))
    x_two = jnp.concatenate([fresh[None], first_out[:-1]], axis=0)
    d_two = jnp.concatenate([first_grad[1:], loss_grad[None]], axis=0)
    second_out, second_grad, gain_two, qgain_two = lax.map(one_slot, (x_two, parked_in[::-1], d_two, gain, qgain, lengths[2 * section_count - section_ids], lengths[section_ids + 1]))
    return (second_out, second_grad, x_two[::-1], gain_one + gain_two, qgain_one + qgain_two)
```

```python
import functools

import jax
import jax.numpy as jnp
from jax import lax
from jax.experimental import pallas as pl
from jax.experimental.pallas import tpu as pltpu
from jax.sharding import PartitionSpec as P

D = 12288
HD = 128
TOK = 256
HALF = 128
EPSILON = 1e-05
LOG2E = 1.4426950408889634
MASKED = -1e30
VMEM_LIMIT = 40 * 1024 * 1024
UNROLL = 6
COST = 1.0
MIRROR_ROWS = (256,)
AFTER = ((), (), ('m0', 'tm', 'x', ), (), (), (), ())
PARK_ROWS = (256,)
LAST = True

ROWS_ROWS = (((1,), (1,)), ((), ()))
COLS_ROWS = (((0,), (0,)), ((), ()))
PLAIN = (((1,), (0,)), ((), ()))


def matmul(left, right, dims):
    return lax.dot_general(left, right, dims, preferred_element_type=jnp.float32)


def token_row(per_lane):
    return jnp.sum(per_lane.T, axis=0, keepdims=True)


def token_columns(row):
    return jnp.broadcast_to(row, (HD, TOK)).T


def gathered_row(sums_ref, k):
    return jnp.sum(sums_ref[:, k, :], axis=0, keepdims=True)


def inverse_rms(sum_row):
    return lax.rsqrt(sum_row / D + EPSILON)


def head_columns(h):
    return pl.ds(pl.multiple_of(h * HD, HD), HD)


def over_heads(count, body, init=None):
    def step(i, carry):
        for u in range(UNROLL):
            carry = body(i * UNROLL + u, carry)
        return carry

    return lax.fori_loop(0, count // UNROLL, step, init)


def fill_bias(bias, length):
    key = lax.broadcasted_iota(jnp.int32, (TOK, TOK), 0)
    query = lax.broadcasted_iota(jnp.int32, (TOK, TOK), 1)
    bias[...] = jnp.where((key <= query) & (key < length), 0.0, MASKED)


def attention(hidden, query, bias):
    low = matmul(hidden[:HALF], query, ROWS_ROWS) + bias[:HALF, :]
    high = matmul(hidden[HALF:], query[HALF:], ROWS_ROWS) + bias[HALF:, HALF:]
    top_low = jnp.max(low, axis=0, keepdims=True)
    top_high = jnp.maximum(top_low[:, HALF:], jnp.max(high, axis=0, keepdims=True))
    top = jnp.concatenate([top_low[:, :HALF], top_high], axis=1)
    low = jnp.exp2((low - top) * LOG2E)
    high = jnp.exp2((high - top_high) * LOG2E)
    total_low = jnp.sum(low, axis=0, keepdims=True)
    total_high = total_low[:, HALF:] + jnp.sum(high, axis=0, keepdims=True)
    scale_high = 1.0 / total_high
    scale = jnp.concatenate([1.0 / total_low[:, :HALF], scale_high], axis=1)
    return low * scale, high * scale_high


def over_queries(low, high, right):
    first = matmul(low[:, :HALF], right[:HALF], COLS_ROWS)
    second = matmul(jnp.concatenate([low[:, HALF:], high], axis=0), right, COLS_ROWS)
    return jnp.concatenate([first, second], axis=0)


def squares(ref):
    total = None
    for h in range(ref.shape[1] // HD):
        block = ref[:, h * HD : (h + 1) * HD].astype(jnp.float32)
        total = block * block if total is None else total + block * block
    return token_row(total)


def put_rows(out_ref, rows):
    stacked = jnp.concatenate(rows + [jnp.zeros((8 - len(rows), TOK), jnp.float32)], axis=0)
    out_ref[...] = jnp.broadcast_to(stacked[None], out_ref.shape)


def squares_kernel(x_ref, stored_ref, parked_ref, out_ref):
    put_rows(out_ref, [squares(x_ref), squares(stored_ref), squares(parked_ref)])


def forward_kernel(micro, pick, select, len_ref, x_ref, sums_ref, gain_ref, qgain_ref, *rest):
    if select:
        other_ref, y_ref, squares_ref, inv, bias, total = rest
    else:
        y_ref, inv, bias = rest
    if pick is None:
        row = sums_ref[0:1, :]
    else:
        row = gathered_row(sums_ref, pick)
    inv[...] = token_columns(inverse_rms(row))
    fill_bias(bias, len_ref[micro(lax.axis_index("section"))])
    if select:
        total[...] = jnp.zeros_like(total)

    def body(h, carry):
        cols = head_columns(h)
        x = x_ref[:, cols].astype(jnp.float32)
        normed = x * inv[...] * gain_ref[0:1, cols]
        hidden = normed.astype(jnp.bfloat16)
        query = (normed * (qgain_ref[0:1, cols] * (1.0 / HD))).astype(jnp.bfloat16)
        low, high = attention(hidden, query, bias)
        mixed = over_queries(low.astype(jnp.bfloat16), high.astype(jnp.bfloat16), hidden)
        y = (x + mixed).astype(jnp.bfloat16)
        if select:
            y = jnp.where(lax.axis_index("section") == lax.axis_size("section") - 1, other_ref[:, cols], y)
            y_float = y.astype(jnp.float32)
            total[...] += y_float * y_float
        y_ref[:, cols] = y
        return carry

    over_heads(x_ref.shape[1] // HD, body)
    if select:
        squares_ref[...] = jnp.broadcast_to(token_row(total[...]), squares_ref.shape)


def rows_of(refs, cols):
    return jnp.concatenate([r[:, cols].astype(jnp.float32) for r in refs], axis=0)


def backward_kernel(micro, pick, first, parts, len_ref, *rest):
    x_refs, (dy_ref, sums_ref, gain_ref, qgain_ref), rest = rest[:parts], rest[parts : parts + 4], rest[parts + 4 :]
    if first:
        extra_ref, d_unit_ref, sums_out_ref, gain_out, qgain_out, inv, bias, total = rest
    else:
        gain_in, qgain_in, d_unit_ref, sums_out_ref, gain_out, qgain_out, inv, bias, total = rest
    if pick is None:
        row = sums_ref[0:1, :]
    else:
        row = gathered_row(sums_ref, pick)
    inv[...] = token_columns(inverse_rms(row))
    fill_bias(bias, len_ref[micro(lax.axis_index("section"))])
    total[...] = jnp.zeros_like(total)

    def body(h, carry):
        cols = head_columns(h)
        unit = rows_of(x_refs, cols) * inv[...]
        gain = gain_ref[0:1, cols]
        small_qgain = qgain_ref[0:1, cols] * (1.0 / HD)
        normed = unit * gain
        hidden = normed.astype(jnp.bfloat16)
        query = (normed * small_qgain).astype(jnp.bfloat16)
        dy = dy_ref[:, cols]
        low, high = attention(hidden, query, bias)
        d_low = matmul(hidden[:HALF], dy, ROWS_ROWS)
        d_high = matmul(hidden[HALF:], dy[HALF:], ROWS_ROWS)
        mean_low = jnp.sum(low * d_low, axis=0, keepdims=True)
        mean_high = mean_low[:, HALF:] + jnp.sum(high * d_high, axis=0, keepdims=True)
        mean = jnp.concatenate([mean_low[:, :HALF], mean_high], axis=1)
        ds_low = (low * (d_low - mean)).astype(jnp.bfloat16)
        ds_high = (high * (d_high - mean_high)).astype(jnp.bfloat16)
        low = low.astype(jnp.bfloat16)
        high = high.astype(jnp.bfloat16)
        first_keys = matmul(
            jnp.concatenate([ds_low, low], axis=1), jnp.concatenate([query, dy], axis=0), PLAIN
        )
        last_keys = matmul(
            jnp.concatenate([ds_high, high], axis=1),
            jnp.concatenate([query[HALF:], dy[HALF:]], axis=0),
            PLAIN,
        )
        d_query = over_queries(ds_low, ds_high, hidden)
        d_normed = d_query * small_qgain + jnp.concatenate([first_keys, last_keys], axis=0)
        qgain_part = jnp.sum(d_query * normed, axis=0, keepdims=True) * (1.0 / HD)
        along = d_normed * unit
        gain_part = jnp.sum(along, axis=0, keepdims=True)
        if not first:
            qgain_part = qgain_part + qgain_in[0:1, cols]
            gain_part = gain_part + gain_in[0:1, cols]
        qgain_out[0:1, cols] = qgain_part
        gain_out[0:1, cols] = gain_part
        total[...] += along * gain
        d_unit_ref[:, cols] = d_normed * gain
        return carry

    over_heads(dy_ref.shape[1] // HD, body)
    rows = [token_row(total[...])]
    if first:
        rows.append(extra_ref[0:1, :])
    put_rows(sums_out_ref, rows)


def finish_kernel(pick, first, parts, flag_ref, *rest):
    x_refs, (dy_ref, d_unit_ref, sums_ref, project_ref), rest = rest[:parts], rest[parts : parts + 4], rest[parts + 4 :]
    if first:
        other_ref, out_ref, passed_ref, inv, project = rest
    else:
        out_ref, inv, project = rest
    if pick is None:
        row = sums_ref[0:1, :]
    else:
        row = gathered_row(sums_ref, pick)
    inv[...] = token_columns(inverse_rms(row))
    project[...] = token_columns(gathered_row(project_ref, 0) / D)
    for h in range(dy_ref.shape[1] // HD):
        cols = slice(h * HD, (h + 1) * HD)
        unit = rows_of(x_refs, cols) * inv[...]
        dx = dy_ref[:, cols].astype(jnp.float32) + inv[...] * (
            d_unit_ref[:, cols] - unit * project[...]
        )
        dx = dx.astype(jnp.bfloat16)
        if first:
            dx = jnp.where(lax.axis_index("section") == 0, other_ref[:, cols], dx)
        out_ref[:, cols] = dx
    if first:
        passed_ref[...] = jnp.broadcast_to(gathered_row(project_ref, 1), passed_ref.shape)


VMEM = pl.BlockSpec(memory_space=pltpu.VMEM)
SMEM = pl.BlockSpec(memory_space=pltpu.SMEM)


def call(kernel, name, args, outs, scratch, flops, smem_first=True, after=()):
    read = sum(a.size * a.dtype.itemsize for a in args)
    written = sum(o.size * o.dtype.itemsize for o in outs)
    def body(*refs):
        kernel(*refs[: len(args)], *refs[len(args) + len(after) :])

    return pl.pallas_call(
        body,
        name=name,
        out_shape=outs,
        in_specs=[SMEM if (smem_first and i == 0) else VMEM for i in range(len(args))]
        + [pl.BlockSpec(memory_space=pl.ANY)] * len(after),
        out_specs=[VMEM] * len(outs),
        scratch_shapes=scratch,
        compiler_params=pltpu.CompilerParams(vmem_limit_bytes=VMEM_LIMIT),
        cost_estimate=pl.CostEstimate(
            flops=int(flops * COST), bytes_accessed=int((read + written) * COST), transcendentals=0
        ),
    )(*args, *after)


def shape(dims, kind):
    return jax.ShapeDtypeStruct(dims, kind)


SUMS = shape((8, 8, TOK), jnp.float32)
COLS = pltpu.VMEM((TOK, HD), jnp.float32)
BIAS = pltpu.VMEM((TOK, TOK), jnp.float32)


def squares_call(x, stored, parked):
    return call(squares_kernel, "squares", [x, stored, parked], [SUMS], [], 10**9, False)[0]


def forward_first(micro, lens, x, sums, gain, qgain, other, after=()):
    outs = [shape(x.shape, jnp.bfloat16), shape((8, TOK), jnp.float32)]
    return call(
        functools.partial(forward_kernel, micro, 0, True), "forward_first",
        [lens, x, sums, gain, qgain, other], outs, [COLS, BIAS, COLS], 3 * 10**9, True, after,
    )


def forward_second(micro, lens, x, sums, gain, qgain, after=()):
    return call(
        functools.partial(forward_kernel, micro, None, False), "forward_second",
        [lens, x, sums, gain, qgain], [shape(x.shape, jnp.bfloat16)], [COLS, BIAS], 3 * 10**9, True, after,
    )[0]


def backward_call(micro, first, lens, x, dy, sums, gain, qgain, rest, after=()):
    outs = [shape(dy.shape, jnp.float32), SUMS, shape(gain.shape, jnp.float32), shape(gain.shape, jnp.float32)]
    return call(
        functools.partial(backward_kernel, micro, 1 if first else None, first, len(x)),
        "backward_first" if first else "backward_second",
        [lens, *x, dy, sums, gain, qgain] + rest, outs, [COLS, BIAS, COLS], 6 * 10**9, True, after,
    )


def finish_call(first, lens, x, dy, d_unit, sums, project, rest, after=()):
    outs = [shape(dy.shape, jnp.bfloat16)]
    if first:
        outs.append(shape((8, TOK), jnp.float32))
    return call(
        functools.partial(finish_kernel, 1 if first else None, first, len(x)),
        "finish_first" if first else "finish_second",
        [lens, *x, dy, d_unit, sums, project] + rest, outs, [COLS, COLS], 10**9, True, after,
    )


def settle_kernel(*refs):
    pass


def settle(parts, after):
    whole = parts[0]
    in_hbm = pl.BlockSpec(memory_space=pltpu.HBM)
    return pl.pallas_call(
        settle_kernel,
        name="settle",
        out_shape=shape(whole.shape, whole.dtype),
        in_specs=[in_hbm] + [pl.BlockSpec(memory_space=pl.ANY)] * len(after),
        out_specs=in_hbm,
        input_output_aliases={0: 0},
    )(whole, *after)


def gathered(sums):
    return lax.all_to_all(sums, "tensor", 0, 0)


def per_device(x_in, grad_in, stash_near, parked_in, fresh, loss_grad, gain, qgain, lengths):
    count = lax.axis_size("section")
    mirrored = [(i, count - 1 - i) for i in range(count)]
    parking = [(i, (count - 2 - i) % count) for i in range(count)]
    onward = [(i, (i + 1) % count) for i in range(count)]
    back = [((i + 1) % count, i) for i in range(count)]
    x, dy, stored, parked = x_in[0], grad_in[0], stash_near[0], parked_in[0]
    fetched = []
    at = 0
    for rows_n in MIRROR_ROWS:
        fetched.append(lax.ppermute(parked[at : at + rows_n], "section", mirrored))
        at += rows_n
    made = {f"m{i}": v for i, v in enumerate(fetched)}

    def after(k):
        return [made[n] for n in AFTER[k]]

    sums = gathered(squares_call(x, stored, parked))
    stored_squares = jnp.sum(sums[:, 2, :], axis=0, keepdims=True)
    stored_squares = lax.ppermute(jnp.broadcast_to(stored_squares, (8, TOK)), "section", mirrored)
    made["tm"] = stored_squares
    first_out, first_squares = forward_first(
        lambda s: 2 * count - 1 - s, lengths, x, sums, gain, qgain, fresh, after(0)
    )
    x_two = lax.ppermute(first_out, "section", onward)
    parked_out = []
    at = 0
    for i, rows_n in enumerate(PARK_ROWS):
        parked_out.append(lax.ppermute(first_out[at : at + rows_n], "section", parking))
        made[f"p{i}"] = parked_out[-1]
        at += rows_n
    made["x"] = x_two
    d_unit, project, gain_one, qgain_one = backward_call(
        lambda s: s, True, lengths, [stored], dy, sums, gain, qgain, [first_squares], after(1)
    )
    project = gathered(project)
    first_grad, passed = finish_call(
        True, lengths, [stored], dy, d_unit, sums, project, [loss_grad], after(2)
    )
    d_two = lax.ppermute(first_grad, "section", back)
    two_squares = lax.ppermute(passed, "section", onward)
    second_out = forward_second(
        lambda s: 2 * count - s, lengths, x_two, two_squares, gain, qgain, after(4)
    )
    d_unit, project, gain_two, qgain_two = backward_call(
        lambda s: s + 1, False, lengths, fetched, d_two, stored_squares, gain, qgain, [gain_one, qgain_one], after(3)
    )
    project = gathered(project)
    second_grad = finish_call(False, lengths, fetched, d_two, d_unit, stored_squares, project, [], after(5))[0]
    parked_out = settle(parked_out, [made[n] for n in AFTER[6]] + ([second_grad] if LAST else []))
    return (
        second_out[None],
        second_grad[None],
        parked_out[None],
        gain_two,
        qgain_two,
    )


def solution(mesh):
    wide = P("section", None, "tensor")
    narrow = P(None, "tensor")
    rows = P("section", "tensor")
    return jax.shard_map(
        per_device,
        mesh=mesh,
        in_specs=(wide, wide, wide, wide, narrow, narrow, rows, rows, P()),
        out_specs=(wide, wide, wide, rows, rows),
        check_vma=False,
    )
```

```python
import functools

import jax
import jax.numpy as jnp
from jax import lax
from jax.experimental import pallas as pl
from jax.experimental.pallas import tpu as pltpu
from jax.sharding import PartitionSpec as P

D = 12288
HD = 128
TOK = 256
HALF = 128
EPSILON = 1e-05
LOG2E = 1.4426950408889634
MASKED = -1e30
VMEM_LIMIT = 40 * 1024 * 1024
WHOLE_VMEM = 62 * 1024 * 1024
UNROLL = 6
COST = 1.0
AFTER = ((), (), (), ('m', 'tm', ), (), (), ())
LAST = True
HOLD = True

ROWS_ROWS = (((1,), (1,)), ((), ()))
COLS_ROWS = (((0,), (0,)), ((), ()))
PLAIN = (((1,), (0,)), ((), ()))


def matmul(left, right, dims):
    return lax.dot_general(left, right, dims, preferred_element_type=jnp.float32)


def token_row(per_lane):
    return jnp.sum(per_lane.T, axis=0, keepdims=True)


def token_columns(row):
    return jnp.broadcast_to(row, (HD, TOK)).T


def gathered_row(sums_ref, k):
    return jnp.sum(sums_ref[:, k, :], axis=0, keepdims=True)


def inverse_rms(sum_row):
    return lax.rsqrt(sum_row / D + EPSILON)


def head_columns(h):
    return pl.ds(pl.multiple_of(h * HD, HD), HD)


def over_heads(count, body, init=None):
    def step(i, carry):
        for u in range(UNROLL):
            carry = body(i * UNROLL + u, carry)
        return carry

    return lax.fori_loop(0, count // UNROLL, step, init)


def fill_bias(bias, length):
    key = lax.broadcasted_iota(jnp.int32, (TOK, TOK), 0)
    query = lax.broadcasted_iota(jnp.int32, (TOK, TOK), 1)
    bias[...] = jnp.where((key <= query) & (key < length), 0.0, MASKED)


def attention(hidden, query, bias):
    low = matmul(hidden[:HALF], query, ROWS_ROWS) + bias[:HALF, :]
    high = matmul(hidden[HALF:], query[HALF:], ROWS_ROWS) + bias[HALF:, HALF:]
    top_low = jnp.max(low, axis=0, keepdims=True)
    top_high = jnp.maximum(top_low[:, HALF:], jnp.max(high, axis=0, keepdims=True))
    top = jnp.concatenate([top_low[:, :HALF], top_high], axis=1)
    low = jnp.exp2((low - top) * LOG2E)
    high = jnp.exp2((high - top_high) * LOG2E)
    total_low = jnp.sum(low, axis=0, keepdims=True)
    total_high = total_low[:, HALF:] + jnp.sum(high, axis=0, keepdims=True)
    scale_high = 1.0 / total_high
    scale = jnp.concatenate([1.0 / total_low[:, :HALF], scale_high], axis=1)
    return low * scale, high * scale_high


def over_queries(low, high, right):
    first = matmul(low[:, :HALF], right[:HALF], COLS_ROWS)
    second = matmul(jnp.concatenate([low[:, HALF:], high], axis=0), right, COLS_ROWS)
    return jnp.concatenate([first, second], axis=0)


def squares(ref):
    total = None
    for h in range(ref.shape[1] // HD):
        block = ref[:, h * HD : (h + 1) * HD].astype(jnp.float32)
        total = block * block if total is None else total + block * block
    return token_row(total)


def put_rows(out_ref, rows):
    stacked = jnp.concatenate(rows + [jnp.zeros((8 - len(rows), TOK), jnp.float32)], axis=0)
    out_ref[...] = jnp.broadcast_to(stacked[None], out_ref.shape)


def squares_kernel(x_ref, stored_ref, parked_ref, out_ref, held, arrived):
    refs = (x_ref, stored_ref, parked_ref)
    copies = [pltpu.make_async_copy(r, held.at[k], arrived.at[k]) for k, r in enumerate(refs)]
    for copy in copies:
        copy.start()
    rows = []
    for k, copy in enumerate(copies):
        copy.wait()
        rows.append(squares(held.at[k]))
    put_rows(out_ref, rows)


def forward_kernel(micro, pick, select, len_ref, x_ref, sums_ref, gain_ref, qgain_ref, *rest):
    if select:
        other_ref, y_ref, copy_ref, inv, bias = rest
    else:
        y_ref, inv, bias = rest
    if pick is None:
        row = sums_ref[0:1, :]
    else:
        row = gathered_row(sums_ref, pick)
    inv[...] = token_columns(inverse_rms(row))
    fill_bias(bias, len_ref[micro(lax.axis_index("section"))])
    def body(h, carry):
        cols = head_columns(h)
        x = x_ref[:, cols].astype(jnp.float32)
        normed = x * inv[...] * gain_ref[0:1, cols]
        hidden = normed.astype(jnp.bfloat16)
        query = (normed * (qgain_ref[0:1, cols] * (1.0 / HD))).astype(jnp.bfloat16)
        low, high = attention(hidden, query, bias)
        mixed = over_queries(low.astype(jnp.bfloat16), high.astype(jnp.bfloat16), hidden)
        y = (x + mixed).astype(jnp.bfloat16)
        if select:
            y = jnp.where(lax.axis_index("section") == lax.axis_size("section") - 1, other_ref[:, cols], y)
        y_ref[:, cols] = y
        if select:
            copy_ref[:, cols] = y
        return carry

    over_heads(x_ref.shape[1] // HD, body)


def rows_of(refs, cols):
    return jnp.concatenate([r[:, cols].astype(jnp.float32) for r in refs], axis=0)


def backward_kernel(micro, pick, first, parts, len_ref, *rest):
    x_refs, (dy_ref, sums_ref, gain_ref, qgain_ref), rest = rest[:parts], rest[parts : parts + 4], rest[parts + 4 :]
    if first:
        d_unit_ref, sums_out_ref, gain_out, qgain_out, inv, bias, total = rest
    else:
        gain_in, qgain_in, next_ref, d_unit_ref, sums_out_ref, gain_out, qgain_out, inv, bias, total = rest
    if pick is None:
        row = sums_ref[0:1, :]
    else:
        row = gathered_row(sums_ref, pick)
    inv[...] = token_columns(inverse_rms(row))
    fill_bias(bias, len_ref[micro(lax.axis_index("section"))])
    total[...] = jnp.zeros_like(total)

    def body(h, carry):
        cols = head_columns(h)
        unit = rows_of(x_refs, cols) * inv[...]
        gain = gain_ref[0:1, cols]
        small_qgain = qgain_ref[0:1, cols] * (1.0 / HD)
        normed = unit * gain
        hidden = normed.astype(jnp.bfloat16)
        query = (normed * small_qgain).astype(jnp.bfloat16)
        dy = dy_ref[:, cols]
        low, high = attention(hidden, query, bias)
        d_low = matmul(hidden[:HALF], dy, ROWS_ROWS)
        d_high = matmul(hidden[HALF:], dy[HALF:], ROWS_ROWS)
        mean_low = jnp.sum(low * d_low, axis=0, keepdims=True)
        mean_high = mean_low[:, HALF:] + jnp.sum(high * d_high, axis=0, keepdims=True)
        mean = jnp.concatenate([mean_low[:, :HALF], mean_high], axis=1)
        ds_low = (low * (d_low - mean)).astype(jnp.bfloat16)
        ds_high = (high * (d_high - mean_high)).astype(jnp.bfloat16)
        low = low.astype(jnp.bfloat16)
        high = high.astype(jnp.bfloat16)
        first_keys = matmul(
            jnp.concatenate([ds_low, low], axis=1), jnp.concatenate([query, dy], axis=0), PLAIN
        )
        last_keys = matmul(
            jnp.concatenate([ds_high, high], axis=1),
            jnp.concatenate([query[HALF:], dy[HALF:]], axis=0),
            PLAIN,
        )
        d_query = over_queries(ds_low, ds_high, hidden)
        d_normed = d_query * small_qgain + jnp.concatenate([first_keys, last_keys], axis=0)
        qgain_part = jnp.sum(d_query * normed, axis=0, keepdims=True) * (1.0 / HD)
        along = d_normed * unit
        gain_part = jnp.sum(along, axis=0, keepdims=True)
        if not first:
            qgain_part = qgain_part + qgain_in[0:1, cols]
            gain_part = gain_part + gain_in[0:1, cols]
        qgain_out[0:1, cols] = qgain_part
        gain_out[0:1, cols] = gain_part
        total[...] += along * gain
        d_unit_ref[:, cols] = d_normed * gain
        return carry

    over_heads(dy_ref.shape[1] // HD, body)
    rows = [token_row(total[...])]
    if not first:
        rows.append(squares(next_ref))
    put_rows(sums_out_ref, rows)


def finish_kernel(pick, first, parts, flag_ref, *rest):
    x_refs, (dy_ref, d_unit_ref, sums_ref, project_ref), rest = rest[:parts], rest[parts : parts + 4], rest[parts + 4 :]
    if first:
        other_ref, out_ref, inv, project = rest
    else:
        out_ref, inv, project = rest
    if pick is None:
        row = sums_ref[0:1, :]
    else:
        row = gathered_row(sums_ref, pick)
    inv[...] = token_columns(inverse_rms(row))
    project[...] = token_columns(gathered_row(project_ref, 0) / D)
    for h in range(dy_ref.shape[1] // HD):
        cols = slice(h * HD, (h + 1) * HD)
        unit = rows_of(x_refs, cols) * inv[...]
        dx = dy_ref[:, cols].astype(jnp.float32) + inv[...] * (
            d_unit_ref[:, cols] - unit * project[...]
        )
        dx = dx.astype(jnp.bfloat16)
        if first:
            dx = jnp.where(lax.axis_index("section") == 0, other_ref[:, cols], dx)
        out_ref[:, cols] = dx


VMEM = pl.BlockSpec(memory_space=pltpu.VMEM)
SMEM = pl.BlockSpec(memory_space=pltpu.SMEM)


def call(kernel, name, args, outs, scratch, flops, smem_first=True, after=()):
    read = sum(a.size * a.dtype.itemsize for a in args)
    written = sum(o.size * o.dtype.itemsize for o in outs)
    def body(*refs):
        kernel(*refs[: len(args)], *refs[len(args) + len(after) :])

    return pl.pallas_call(
        body,
        name=name,
        out_shape=outs,
        in_specs=[SMEM if (smem_first and i == 0) else VMEM for i in range(len(args))]
        + [pl.BlockSpec(memory_space=pl.ANY)] * len(after),
        out_specs=[VMEM] * len(outs),
        scratch_shapes=scratch,
        compiler_params=pltpu.CompilerParams(vmem_limit_bytes=VMEM_LIMIT),
        cost_estimate=pl.CostEstimate(
            flops=int(flops * COST), bytes_accessed=int((read + written) * COST), transcendentals=0
        ),
    )(*args, *after)


def shape(dims, kind):
    return jax.ShapeDtypeStruct(dims, kind)


SUMS = shape((8, 8, TOK), jnp.float32)
COLS = pltpu.VMEM((TOK, HD), jnp.float32)
BIAS = pltpu.VMEM((TOK, TOK), jnp.float32)


def squares_call(x, stored, parked):
    return pl.pallas_call(
        squares_kernel,
        name="squares",
        out_shape=SUMS,
        in_specs=[pl.BlockSpec(memory_space=pltpu.HBM)] * 3,
        out_specs=VMEM,
        scratch_shapes=[pltpu.VMEM((3, *x.shape), x.dtype), pltpu.SemaphoreType.DMA((3,))],
        compiler_params=pltpu.CompilerParams(vmem_limit_bytes=WHOLE_VMEM),
    )(x, stored, parked)


def forward_first(micro, lens, x, sums, gain, qgain, other, after=()):
    outs = [shape(x.shape, jnp.bfloat16)] * 2
    return call(
        functools.partial(forward_kernel, micro, 0, True), "forward_first",
        [lens, x, sums, gain, qgain, other], outs, [COLS, BIAS], 3 * 10**9, True, after,
    )


def forward_second(micro, lens, x, sums, gain, qgain, after=()):
    return call(
        functools.partial(forward_kernel, micro, 1, False), "forward_second",
        [lens, x, sums, gain, qgain], [shape(x.shape, jnp.bfloat16)], [COLS, BIAS], 3 * 10**9, True, after,
    )[0]


def backward_call(micro, first, lens, x, dy, sums, gain, qgain, rest, after=()):
    outs = [shape(dy.shape, jnp.float32), SUMS, shape(gain.shape, jnp.float32), shape(gain.shape, jnp.float32)]
    return call(
        functools.partial(backward_kernel, micro, 1 if first else None, first, len(x)),
        "backward_first" if first else "backward_second",
        [lens, *x, dy, sums, gain, qgain] + rest, outs, [COLS, BIAS, COLS], 6 * 10**9, True, after,
    )


def finish_call(first, lens, x, dy, d_unit, sums, project, rest, after=()):
    outs = [shape(dy.shape, jnp.bfloat16)]
    return call(
        functools.partial(finish_kernel, 1 if first else None, first, len(x)),
        "finish_first" if first else "finish_second",
        [lens, *x, dy, d_unit, sums, project] + rest, outs, [COLS, COLS], 10**9, True, after,
    )


def settle_kernel(parts, *refs):
    sources, out, done = refs[:parts], refs[-2], refs[-1]
    copies = []
    at = 0
    for k, source in enumerate(sources):
        rows_n = source.shape[0]
        copies.append(pltpu.make_async_copy(source, out.at[pl.ds(at, rows_n), :], done.at[k]))
        at += rows_n
    for copy in copies:
        copy.start()
    for copy in copies:
        copy.wait()


def settle(parts, after):
    rows_n = sum(part.shape[0] for part in parts)
    return pl.pallas_call(
        functools.partial(settle_kernel, len(parts)),
        name="settle",
        out_shape=shape((rows_n, parts[0].shape[1]), parts[0].dtype),
        in_specs=[VMEM] * len(parts) + [pl.BlockSpec(memory_space=pl.ANY)] * len(after),
        out_specs=pl.BlockSpec(memory_space=pltpu.HBM),
        scratch_shapes=[pltpu.SemaphoreType.DMA((len(parts),))],
    )(*parts, *after)


def hold_kernel(*refs):
    pass


def hold(value, after):
    return pl.pallas_call(
        hold_kernel,
        name="hold",
        out_shape=shape(value.shape, value.dtype),
        in_specs=[pl.BlockSpec(memory_space=pl.ANY)] * (1 + len(after)),
        out_specs=pl.BlockSpec(memory_space=pl.ANY),
        input_output_aliases={0: 0},
    )(value, *after)


def gathered(sums):
    return lax.all_to_all(sums, "tensor", 0, 0)


def per_device(x_in, grad_in, stash_near, parked_in, fresh, loss_grad, gain, qgain, lengths):
    count = lax.axis_size("section")
    mirrored = [(i, count - 1 - i) for i in range(count)]
    parking = [(i, (count - 2 - i) % count) for i in range(count)]
    onward = [(i, (i + 1) % count) for i in range(count)]
    back = [((i + 1) % count, i) for i in range(count)]
    x, dy, stored, parked = x_in[0], grad_in[0], stash_near[0], parked_in[0]
    fetched = [lax.ppermute(parked, "section", mirrored)]
    made = {"m": fetched[0]}

    def after(k):
        return [made[n] for n in AFTER[k]]

    sums = gathered(squares_call(x, stored, parked))
    stored_squares = jnp.sum(sums[:, 2, :], axis=0, keepdims=True)
    stored_squares = lax.ppermute(jnp.broadcast_to(stored_squares, (8, TOK)), "section", mirrored)
    made["tm"] = stored_squares
    d_unit, project, gain_one, qgain_one = backward_call(
        lambda s: s, True, lengths, [stored], dy, sums, gain, qgain, [], after(0)
    )
    project = gathered(project)
    made["a1"] = project
    first_grad = finish_call(
        True, lengths, [stored], dy, d_unit, sums, project, [loss_grad], after(1)
    )[0]
    made["g1"] = first_grad
    d_two = lax.ppermute(first_grad, "section", back)
    made["dx"] = d_two
    first_out, parking_out = forward_first(
        lambda s: 2 * count - 1 - s, lengths, x, sums, gain, qgain, fresh, after(2)
    )
    if HOLD:
        parking_out = hold(parking_out, after(3))
    made["y1"] = first_out
    x_two = lax.ppermute(first_out, "section", onward)
    made["x"] = x_two
    parked_out = [lax.ppermute(parking_out, "section", parking)]
    d_unit, project, gain_two, qgain_two = backward_call(
        lambda s: s + 1, False, lengths, fetched, d_two, stored_squares, gain, qgain,
        [gain_one, qgain_one, x_two], after(4),
    )
    project = gathered(project)
    second_grad = finish_call(
        False, lengths, fetched, d_two, d_unit, stored_squares, project, [], after(5)
    )[0]
    second_out = forward_second(
        lambda s: 2 * count - s, lengths, x_two, project, gain, qgain, after(6)
    )
    parked_out = settle(parked_out, [second_grad, second_out] if LAST else [])
    return (
        second_out[None],
        second_grad[None],
        parked_out[None],
        gain_two,
        qgain_two,
    )


def solution(mesh):
    wide = P("section", None, "tensor")
    narrow = P(None, "tensor")
    rows = P("section", "tensor")
    return jax.shard_map(
        per_device,
        mesh=mesh,
        in_specs=(wide, wide, wide, wide, narrow, narrow, rows, rows, P()),
        out_specs=(wide, wide, wide, rows, rows),
        check_vma=False,
    )
```

```python
import functools

import jax
import jax.numpy as jnp
from jax import lax
from jax.experimental import pallas as pl
from jax.experimental.pallas import tpu as pltpu
from jax.sharding import PartitionSpec as P

D = 12288
HD = 128
TOK = 256
HALF = 128
EPSILON = 1e-05
LOG2E = 1.4426950408889634
MASKED = -1e30
VMEM_LIMIT = 20 * 1024 * 1024
SMALL_VMEM = 2 * 1024 * 1024
WHOLE_VMEM = 62 * 1024 * 1024
UNROLL = 6
COST = 1.0
AFTER = ((), (), (), ("m0", "tm"), (), (), ())
MIRROR_ROWS = (256,)
HOLD = True

ROWS_ROWS = (((1,), (1,)), ((), ()))
COLS_ROWS = (((0,), (0,)), ((), ()))
PLAIN = (((1,), (0,)), ((), ()))


def matmul(left, right, dims):
    return lax.dot_general(left, right, dims, preferred_element_type=jnp.float32)


def token_row(per_lane):
    return jnp.sum(per_lane.T, axis=0, keepdims=True)


def token_columns(row):
    return jnp.broadcast_to(row, (HD, TOK)).T


def gathered_row(sums_ref, k):
    return jnp.sum(sums_ref[:, k, :], axis=0, keepdims=True)


def inverse_rms(sum_row):
    return lax.rsqrt(sum_row / D + EPSILON)


def head_columns(h):
    return pl.ds(pl.multiple_of(h * HD, HD), HD)


def over_heads(count, body, init=None):
    def step(i, carry):
        for u in range(UNROLL):
            carry = body(i * UNROLL + u, carry)
        return carry

    return lax.fori_loop(0, count // UNROLL, step, init)


def fill_bias(bias, length):
    key = lax.broadcasted_iota(jnp.int32, (TOK, TOK), 0)
    query = lax.broadcasted_iota(jnp.int32, (TOK, TOK), 1)
    bias[...] = jnp.where((key <= query) & (key < length), 0.0, MASKED)


def attention(hidden, query, bias):
    low = matmul(hidden[:HALF], query, ROWS_ROWS) + bias[:HALF, :]
    high = matmul(hidden[HALF:], query[HALF:], ROWS_ROWS) + bias[HALF:, HALF:]
    top_low = jnp.max(low, axis=0, keepdims=True)
    top_high = jnp.maximum(top_low[:, HALF:], jnp.max(high, axis=0, keepdims=True))
    top = jnp.concatenate([top_low[:, :HALF], top_high], axis=1)
    low = jnp.exp2((low - top) * LOG2E)
    high = jnp.exp2((high - top_high) * LOG2E)
    total_low = jnp.sum(low, axis=0, keepdims=True)
    total_high = total_low[:, HALF:] + jnp.sum(high, axis=0, keepdims=True)
    scale_high = 1.0 / total_high
    scale = jnp.concatenate([1.0 / total_low[:, :HALF], scale_high], axis=1)
    return low * scale, high * scale_high


def over_queries(low, high, right):
    first = matmul(low[:, :HALF], right[:HALF], COLS_ROWS)
    second = matmul(jnp.concatenate([low[:, HALF:], high], axis=0), right, COLS_ROWS)
    return jnp.concatenate([first, second], axis=0)


def squares(ref):
    total = None
    for h in range(ref.shape[1] // HD):
        block = ref[:, h * HD : (h + 1) * HD].astype(jnp.float32)
        total = block * block if total is None else total + block * block
    return token_row(total)


def put_rows(out_ref, rows):
    stacked = jnp.concatenate(rows + [jnp.zeros((8 - len(rows), TOK), jnp.float32)], axis=0)
    out_ref[...] = jnp.broadcast_to(stacked[None], out_ref.shape)


def squares_kernel(x_ref, stored_ref, parked_ref, out_ref, held, arrived):
    refs = (x_ref, stored_ref, parked_ref)
    copies = [pltpu.make_async_copy(r, held.at[k], arrived.at[k]) for k, r in enumerate(refs)]
    for copy in copies:
        copy.start()
    rows = []
    for k, copy in enumerate(copies):
        copy.wait()
        rows.append(squares(held.at[k]))
    put_rows(out_ref, rows)


def forward_kernel(micro, pick, select, len_ref, x_ref, sums_ref, gain_ref, qgain_ref, *rest):
    if select:
        other_ref, y_ref, copy_ref, inv, bias = rest
    else:
        y_ref, mark_ref, inv, bias = rest
        mark_ref[...] = jnp.zeros_like(mark_ref)
    if pick is None:
        row = sums_ref[0:1, :]
    else:
        row = gathered_row(sums_ref, pick)
    inv[...] = token_columns(inverse_rms(row))
    fill_bias(bias, len_ref[micro(lax.axis_index("section"))])
    def body(h, carry):
        cols = head_columns(h)
        x = x_ref[:, cols].astype(jnp.float32)
        normed = x * inv[...] * gain_ref[0:1, cols]
        hidden = normed.astype(jnp.bfloat16)
        query = (normed * (qgain_ref[0:1, cols] * (1.0 / HD))).astype(jnp.bfloat16)
        low, high = attention(hidden, query, bias)
        mixed = over_queries(low.astype(jnp.bfloat16), high.astype(jnp.bfloat16), hidden)
        y = (x + mixed).astype(jnp.bfloat16)
        if select:
            y = jnp.where(lax.axis_index("section") == lax.axis_size("section") - 1, other_ref[:, cols], y)
        y_ref[:, cols] = y
        if select:
            copy_ref[:, cols] = y
        return carry

    over_heads(x_ref.shape[1] // HD, body)


def rows_of(refs, cols):
    return jnp.concatenate([r[:, cols].astype(jnp.float32) for r in refs], axis=0)


def backward_kernel(micro, pick, first, parts, len_ref, *rest):
    x_refs, (dy_ref, sums_ref, gain_ref, qgain_ref), rest = rest[:parts], rest[parts : parts + 4], rest[parts + 4 :]
    if first:
        d_unit_ref, sums_out_ref, gain_out, qgain_out, inv, bias, total = rest
    else:
        gain_in, qgain_in, next_ref, d_unit_ref, sums_out_ref, gain_out, qgain_out, inv, bias, total = rest
    if pick is None:
        row = sums_ref[0:1, :]
    else:
        row = gathered_row(sums_ref, pick)
    inv[...] = token_columns(inverse_rms(row))
    fill_bias(bias, len_ref[micro(lax.axis_index("section"))])
    total[...] = jnp.zeros_like(total)

    def body(h, carry):
        cols = head_columns(h)
        unit = rows_of(x_refs, cols) * inv[...]
        gain = gain_ref[0:1, cols]
        small_qgain = qgain_ref[0:1, cols] * (1.0 / HD)
        normed = unit * gain
        hidden = normed.astype(jnp.bfloat16)
        query = (normed * small_qgain).astype(jnp.bfloat16)
        dy = dy_ref[:, cols]
        low, high = attention(hidden, query, bias)
        d_low = matmul(hidden[:HALF], dy, ROWS_ROWS)
        d_high = matmul(hidden[HALF:], dy[HALF:], ROWS_ROWS)
        mean_low = jnp.sum(low * d_low, axis=0, keepdims=True)
        mean_high = mean_low[:, HALF:] + jnp.sum(high * d_high, axis=0, keepdims=True)
        mean = jnp.concatenate([mean_low[:, :HALF], mean_high], axis=1)
        ds_low = (low * (d_low - mean)).astype(jnp.bfloat16)
        ds_high = (high * (d_high - mean_high)).astype(jnp.bfloat16)
        low = low.astype(jnp.bfloat16)
        high = high.astype(jnp.bfloat16)
        first_keys = matmul(
            jnp.concatenate([ds_low, low], axis=1), jnp.concatenate([query, dy], axis=0), PLAIN
        )
        last_keys = matmul(
            jnp.concatenate([ds_high, high], axis=1),
            jnp.concatenate([query[HALF:], dy[HALF:]], axis=0),
            PLAIN,
        )
        d_query = over_queries(ds_low, ds_high, hidden)
        d_normed = d_query * small_qgain + jnp.concatenate([first_keys, last_keys], axis=0)
        qgain_part = jnp.sum(d_query * normed, axis=0, keepdims=True) * (1.0 / HD)
        along = d_normed * unit
        gain_part = jnp.sum(along, axis=0, keepdims=True)
        if not first:
            qgain_part = qgain_part + qgain_in[0:1, cols]
            gain_part = gain_part + gain_in[0:1, cols]
        qgain_out[0:1, cols] = qgain_part
        gain_out[0:1, cols] = gain_part
        total[...] += along * gain
        d_unit_ref[:, cols] = d_normed * gain
        return carry

    over_heads(dy_ref.shape[1] // HD, body)
    rows = [token_row(total[...])]
    if not first:
        rows.append(squares(next_ref))
    put_rows(sums_out_ref, rows)


def finish_kernel(pick, first, parts, flag_ref, *rest):
    x_refs, (dy_ref, d_unit_ref, sums_ref, project_ref), rest = rest[:parts], rest[parts : parts + 4], rest[parts + 4 :]
    if first:
        other_ref, out_ref, inv, project = rest
    else:
        out_ref, inv, project = rest
    if pick is None:
        row = sums_ref[0:1, :]
    else:
        row = gathered_row(sums_ref, pick)
    inv[...] = token_columns(inverse_rms(row))
    project[...] = token_columns(gathered_row(project_ref, 0) / D)
    for h in range(dy_ref.shape[1] // HD):
        cols = slice(h * HD, (h + 1) * HD)
        unit = rows_of(x_refs, cols) * inv[...]
        dx = dy_ref[:, cols].astype(jnp.float32) + inv[...] * (
            d_unit_ref[:, cols] - unit * project[...]
        )
        dx = dx.astype(jnp.bfloat16)
        if first:
            dx = jnp.where(lax.axis_index("section") == 0, other_ref[:, cols], dx)
        out_ref[:, cols] = dx


VMEM = pl.BlockSpec(memory_space=pltpu.VMEM)
SMEM = pl.BlockSpec(memory_space=pltpu.SMEM)


def call(kernel, name, args, outs, scratch, flops, smem_first=True, after=()):
    read = sum(a.size * a.dtype.itemsize for a in args)
    written = sum(o.size * o.dtype.itemsize for o in outs)
    def body(*refs):
        kernel(*refs[: len(args)], *refs[len(args) + len(after) :])

    return pl.pallas_call(
        body,
        name=name,
        out_shape=outs,
        in_specs=[SMEM if (smem_first and i == 0) else VMEM for i in range(len(args))]
        + [pl.BlockSpec(memory_space=pl.ANY)] * len(after),
        out_specs=[VMEM] * len(outs),
        scratch_shapes=scratch,
        compiler_params=pltpu.CompilerParams(vmem_limit_bytes=VMEM_LIMIT),
        cost_estimate=pl.CostEstimate(
            flops=int(flops * COST), bytes_accessed=int((read + written) * COST), transcendentals=0
        ),
    )(*args, *after)


def shape(dims, kind):
    return jax.ShapeDtypeStruct(dims, kind)


SUMS = shape((8, 8, TOK), jnp.float32)
COLS = pltpu.VMEM((TOK, HD), jnp.float32)
BIAS = pltpu.VMEM((TOK, TOK), jnp.float32)


def squares_call(x, stored, parked):
    return pl.pallas_call(
        squares_kernel,
        name="squares",
        out_shape=SUMS,
        in_specs=[pl.BlockSpec(memory_space=pltpu.HBM)] * 3,
        out_specs=VMEM,
        scratch_shapes=[pltpu.VMEM((3, *x.shape), x.dtype), pltpu.SemaphoreType.DMA((3,))],
        compiler_params=pltpu.CompilerParams(vmem_limit_bytes=WHOLE_VMEM),
    )(x, stored, parked)


def forward_first(micro, lens, x, sums, gain, qgain, other, after=()):
    outs = [shape(x.shape, jnp.bfloat16)] * 2
    return call(
        functools.partial(forward_kernel, micro, 0, True), "forward_first",
        [lens, x, sums, gain, qgain, other], outs, [COLS, BIAS], 3 * 10**9, True, after,
    )


def forward_second(micro, lens, x, sums, gain, qgain, after=()):
    return call(
        functools.partial(forward_kernel, micro, 1, False), "forward_second",
        [lens, x, sums, gain, qgain], [shape(x.shape, jnp.bfloat16), shape((8, HD), jnp.float32)], [COLS, BIAS], 3 * 10**9, True, after,
    )


def backward_call(micro, first, lens, x, dy, sums, gain, qgain, rest, after=()):
    outs = [shape(dy.shape, jnp.float32), SUMS, shape(gain.shape, jnp.float32), shape(gain.shape, jnp.float32)]
    return call(
        functools.partial(backward_kernel, micro, 1 if first else None, first, len(x)),
        "backward_first" if first else "backward_second",
        [lens, *x, dy, sums, gain, qgain] + rest, outs, [COLS, BIAS, COLS], 6 * 10**9, True, after,
    )


def finish_call(first, lens, x, dy, d_unit, sums, project, rest, after=()):
    outs = [shape(dy.shape, jnp.bfloat16)]
    return call(
        functools.partial(finish_kernel, 1 if first else None, first, len(x)),
        "finish_first" if first else "finish_second",
        [lens, *x, dy, d_unit, sums, project] + rest, outs, [COLS, COLS], 10**9, True, after,
    )


def settle_kernel(parts, *refs):
    sources, out, done = refs[:parts], refs[-2], refs[-1]
    copies = []
    at = 0
    for k, source in enumerate(sources):
        rows_n = source.shape[0]
        copies.append(pltpu.make_async_copy(source, out.at[pl.ds(at, rows_n), :], done.at[k]))
        at += rows_n
    for copy in copies:
        copy.start()
    for copy in copies:
        copy.wait()


def settle(parts, after):
    rows_n = sum(part.shape[0] for part in parts)
    return pl.pallas_call(
        functools.partial(settle_kernel, len(parts)),
        name="settle",
        out_shape=shape((rows_n, parts[0].shape[1]), parts[0].dtype),
        in_specs=[VMEM] * len(parts) + [pl.BlockSpec(memory_space=pl.ANY)] * len(after),
        out_specs=pl.BlockSpec(memory_space=pltpu.HBM),
        scratch_shapes=[pltpu.SemaphoreType.DMA((len(parts),))],
        compiler_params=pltpu.CompilerParams(vmem_limit_bytes=SMALL_VMEM),
    )(*parts, *after)


def hold_kernel(*refs):
    pass


def hold(value, after):
    return pl.pallas_call(
        hold_kernel,
        name="hold",
        out_shape=shape(value.shape, value.dtype),
        in_specs=[pl.BlockSpec(memory_space=pl.ANY)] * (1 + len(after)),
        out_specs=pl.BlockSpec(memory_space=pl.ANY),
        input_output_aliases={0: 0},
        compiler_params=pltpu.CompilerParams(vmem_limit_bytes=SMALL_VMEM),
    )(value, *after)


def gathered(sums):
    return lax.all_to_all(sums, "tensor", 0, 0)


def per_device(x_in, grad_in, stash_near, parked_in, fresh, loss_grad, gain, qgain, lengths):
    count = lax.axis_size("section")
    mirrored = [(i, count - 1 - i) for i in range(count)]
    parking = [(i, (count - 2 - i) % count) for i in range(count)]
    onward = [(i, (i + 1) % count) for i in range(count)]
    back = [((i + 1) % count, i) for i in range(count)]
    x, dy, stored, parked = x_in[0], grad_in[0], stash_near[0], parked_in[0]
    fetched = []
    at = 0
    for rows_n in MIRROR_ROWS:
        fetched.append(lax.ppermute(parked[at : at + rows_n], "section", mirrored))
        at += rows_n
    made = {f"m{i}": part for i, part in enumerate(fetched)}

    def after(k):
        return [made[n] for n in AFTER[k]]

    sums = gathered(squares_call(x, stored, parked))
    stored_squares = jnp.sum(sums[:, 2, :], axis=0, keepdims=True)
    stored_squares = lax.ppermute(jnp.broadcast_to(stored_squares, (8, TOK)), "section", mirrored)
    made["tm"] = stored_squares
    d_unit, project, gain_one, qgain_one = backward_call(
        lambda s: s, True, lengths, [stored], dy, sums, gain, qgain, [], after(0)
    )
    project = gathered(project)
    made["a1"] = project
    first_grad = finish_call(
        True, lengths, [stored], dy, d_unit, sums, project, [loss_grad], after(1)
    )[0]
    made["g1"] = first_grad
    d_two = lax.ppermute(first_grad, "section", back)
    made["dx"] = d_two
    first_out, parking_out = forward_first(
        lambda s: 2 * count - 1 - s, lengths, x, sums, gain, qgain, fresh, after(2)
    )
    if HOLD:
        parking_out = hold(parking_out, after(3))
    made["y1"] = first_out
    x_two = lax.ppermute(first_out, "section", onward)
    made["x"] = x_two
    parked_out = [lax.ppermute(parking_out, "section", parking)]
    d_unit, project, gain_two, qgain_two = backward_call(
        lambda s: s + 1, False, lengths, fetched, d_two, stored_squares, gain, qgain,
        [gain_one, qgain_one, x_two], after(4),
    )
    project = gathered(project)
    second_grad = finish_call(
        False, lengths, fetched, d_two, d_unit, stored_squares, project, [], after(5)
    )[0]
    second_out, mark = forward_second(
        lambda s: 2 * count - s, lengths, x_two, project, gain, qgain, after(6)
    )
    parked_out = settle(parked_out, [mark])
    return (
        second_out[None],
        second_grad[None],
        parked_out[None],
        gain_two,
        qgain_two,
    )


def solution(mesh):
    wide = P("section", None, "tensor")
    narrow = P(None, "tensor")
    rows = P("section", "tensor")
    return jax.shard_map(
        per_device,
        mesh=mesh,
        in_specs=(wide, wide, wide, wide, narrow, narrow, rows, rows, P()),
        out_specs=(wide, wide, wide, rows, rows),
        check_vma=False,
    )
```

```python
import functools

import jax
import jax.numpy as jnp
from jax import lax
from jax.experimental import pallas as pl
from jax.experimental.pallas import tpu as pltpu
from jax.sharding import PartitionSpec as P

D = 12288
HD = 128
TOK = 256
HALF = 128
EPSILON = 1e-05
LOG2E = 1.4426950408889634
MASKED = -1e30
VMEM_LIMIT = 20 * 1024 * 1024
SMALL_VMEM = 2 * 1024 * 1024
WHOLE_VMEM = 62 * 1024 * 1024
UNROLL = 12
COST = 1.0
AFTER = ((), (), (), ("m0", "tm"), (), (), ())
MIRROR_ROWS = (256,)
HOLD = True

ROWS_ROWS = (((1,), (1,)), ((), ()))
COLS_ROWS = (((0,), (0,)), ((), ()))
PLAIN = (((1,), (0,)), ((), ()))


def matmul(left, right, dims):
    return lax.dot_general(left, right, dims, preferred_element_type=jnp.float32)


def token_row(per_lane):
    return jnp.sum(per_lane.T, axis=0, keepdims=True)


def token_columns(row):
    return jnp.broadcast_to(row, (HD, TOK)).T


def gathered_row(sums_ref, k):
    return jnp.sum(sums_ref[:, k, :], axis=0, keepdims=True)


def inverse_rms(sum_row):
    return lax.rsqrt(sum_row / D + EPSILON)


def head_columns(h):
    return pl.ds(pl.multiple_of(h * HD, HD), HD)


def over_heads(count, body, init=None):
    def step(i, carry):
        for u in range(UNROLL):
            carry = body(i * UNROLL + u, carry)
        return carry

    return lax.fori_loop(0, count // UNROLL, step, init)


def fill_bias(bias, length):
    key = lax.broadcasted_iota(jnp.int32, (TOK, TOK), 0)
    query = lax.broadcasted_iota(jnp.int32, (TOK, TOK), 1)
    bias[...] = jnp.where((key <= query) & (key < length), 0.0, MASKED)


def attention(hidden, query, bias):
    low = matmul(hidden[:HALF], query, ROWS_ROWS) + bias[:HALF, :]
    high = matmul(hidden[HALF:], query[HALF:], ROWS_ROWS) + bias[HALF:, HALF:]
    top_low = jnp.max(low, axis=0, keepdims=True)
    top_high = jnp.maximum(top_low[:, HALF:], jnp.max(high, axis=0, keepdims=True))
    top = jnp.concatenate([top_low[:, :HALF], top_high], axis=1)
    low = jnp.exp2((low - top) * LOG2E)
    high = jnp.exp2((high - top_high) * LOG2E)
    total_low = jnp.sum(low, axis=0, keepdims=True)
    total_high = total_low[:, HALF:] + jnp.sum(high, axis=0, keepdims=True)
    scale_high = 1.0 / total_high
    scale = jnp.concatenate([1.0 / total_low[:, :HALF], scale_high], axis=1)
    return low * scale, high * scale_high


def over_queries(low, high, right):
    first = matmul(low[:, :HALF], right[:HALF], COLS_ROWS)
    second = matmul(jnp.concatenate([low[:, HALF:], high], axis=0), right, COLS_ROWS)
    return jnp.concatenate([first, second], axis=0)


def squares(ref):
    total = None
    for h in range(ref.shape[1] // HD):
        block = ref[:, h * HD : (h + 1) * HD].astype(jnp.float32)
        total = block * block if total is None else total + block * block
    return token_row(total)


def put_rows(out_ref, rows):
    stacked = jnp.concatenate(rows + [jnp.zeros((8 - len(rows), TOK), jnp.float32)], axis=0)
    out_ref[...] = jnp.broadcast_to(stacked[None], out_ref.shape)


def squares_kernel(x_ref, stored_ref, parked_ref, out_ref, held, arrived):
    refs = (x_ref, stored_ref, parked_ref)
    copies = [pltpu.make_async_copy(r, held.at[k], arrived.at[k]) for k, r in enumerate(refs)]
    for copy in copies:
        copy.start()
    rows = []
    for k, copy in enumerate(copies):
        copy.wait()
        rows.append(squares(held.at[k]))
    put_rows(out_ref, rows)


def forward_kernel(micro, pick, select, len_ref, x_ref, sums_ref, gain_ref, qgain_ref, *rest):
    if select:
        other_ref, y_ref, copy_ref, inv, bias = rest
    else:
        y_ref, mark_ref, inv, bias = rest
        mark_ref[...] = jnp.zeros_like(mark_ref)
    if pick is None:
        row = sums_ref[0:1, :]
    else:
        row = gathered_row(sums_ref, pick)
    inv[...] = token_columns(inverse_rms(row))
    fill_bias(bias, len_ref[micro(lax.axis_index("section"))])
    def body(h, carry):
        cols = head_columns(h)
        x = x_ref[:, cols].astype(jnp.float32)
        normed = x * inv[...] * gain_ref[0:1, cols]
        hidden = normed.astype(jnp.bfloat16)
        query = (normed * (qgain_ref[0:1, cols] * (1.0 / HD))).astype(jnp.bfloat16)
        low, high = attention(hidden, query, bias)
        mixed = over_queries(low.astype(jnp.bfloat16), high.astype(jnp.bfloat16), hidden)
        y = (x + mixed).astype(jnp.bfloat16)
        if select:
            y = jnp.where(lax.axis_index("section") == lax.axis_size("section") - 1, other_ref[:, cols], y)
        y_ref[:, cols] = y
        if select:
            copy_ref[:, cols] = y
        return carry

    over_heads(x_ref.shape[1] // HD, body)


def rows_of(refs, cols):
    return jnp.concatenate([r[:, cols].astype(jnp.float32) for r in refs], axis=0)


def backward_kernel(micro, pick, first, parts, len_ref, *rest):
    x_refs, (dy_ref, sums_ref, gain_ref, qgain_ref), rest = rest[:parts], rest[parts : parts + 4], rest[parts + 4 :]
    if first:
        d_unit_ref, sums_out_ref, gain_out, qgain_out, inv, bias, total = rest
    else:
        gain_in, qgain_in, next_ref, d_unit_ref, sums_out_ref, gain_out, qgain_out, inv, bias, total = rest
    if pick is None:
        row = sums_ref[0:1, :]
    else:
        row = gathered_row(sums_ref, pick)
    inv[...] = token_columns(inverse_rms(row))
    fill_bias(bias, len_ref[micro(lax.axis_index("section"))])
    total[...] = jnp.zeros_like(total)

    def body(h, carry):
        cols = head_columns(h)
        unit = rows_of(x_refs, cols) * inv[...]
        gain = gain_ref[0:1, cols]
        small_qgain = qgain_ref[0:1, cols] * (1.0 / HD)
        normed = unit * gain
        hidden = normed.astype(jnp.bfloat16)
        query = (normed * small_qgain).astype(jnp.bfloat16)
        dy = dy_ref[:, cols]
        low, high = attention(hidden, query, bias)
        d_low = matmul(hidden[:HALF], dy, ROWS_ROWS)
        d_high = matmul(hidden[HALF:], dy[HALF:], ROWS_ROWS)
        mean_low = jnp.sum(low * d_low, axis=0, keepdims=True)
        mean_high = mean_low[:, HALF:] + jnp.sum(high * d_high, axis=0, keepdims=True)
        mean = jnp.concatenate([mean_low[:, :HALF], mean_high], axis=1)
        ds_low = (low * (d_low - mean)).astype(jnp.bfloat16)
        ds_high = (high * (d_high - mean_high)).astype(jnp.bfloat16)
        low = low.astype(jnp.bfloat16)
        high = high.astype(jnp.bfloat16)
        first_keys = matmul(
            jnp.concatenate([ds_low, low], axis=1), jnp.concatenate([query, dy], axis=0), PLAIN
        )
        last_keys = matmul(
            jnp.concatenate([ds_high, high], axis=1),
            jnp.concatenate([query[HALF:], dy[HALF:]], axis=0),
            PLAIN,
        )
        d_query = over_queries(ds_low, ds_high, hidden)
        d_normed = d_query * small_qgain + jnp.concatenate([first_keys, last_keys], axis=0)
        qgain_part = jnp.sum(d_query * normed, axis=0, keepdims=True) * (1.0 / HD)
        along = d_normed * unit
        gain_part = jnp.sum(along, axis=0, keepdims=True)
        if not first:
            qgain_part = qgain_part + qgain_in[0:1, cols]
            gain_part = gain_part + gain_in[0:1, cols]
        qgain_out[0:1, cols] = qgain_part
        gain_out[0:1, cols] = gain_part
        total[...] += along * gain
        d_unit_ref[:, cols] = d_normed * gain
        return carry

    over_heads(dy_ref.shape[1] // HD, body)
    rows = [token_row(total[...])]
    if not first:
        rows.append(squares(next_ref))
    put_rows(sums_out_ref, rows)


def finish_kernel(pick, first, parts, flag_ref, *rest):
    x_refs, (dy_ref, d_unit_ref, sums_ref, project_ref), rest = rest[:parts], rest[parts : parts + 4], rest[parts + 4 :]
    if first:
        other_ref, out_ref, inv, project = rest
    else:
        out_ref, inv, project = rest
    if pick is None:
        row = sums_ref[0:1, :]
    else:
        row = gathered_row(sums_ref, pick)
    inv[...] = token_columns(inverse_rms(row))
    project[...] = token_columns(gathered_row(project_ref, 0) / D)
    for h in range(dy_ref.shape[1] // HD):
        cols = slice(h * HD, (h + 1) * HD)
        unit = rows_of(x_refs, cols) * inv[...]
        dx = dy_ref[:, cols].astype(jnp.float32) + inv[...] * (
            d_unit_ref[:, cols] - unit * project[...]
        )
        dx = dx.astype(jnp.bfloat16)
        if first:
            dx = jnp.where(lax.axis_index("section") == 0, other_ref[:, cols], dx)
        out_ref[:, cols] = dx


VMEM = pl.BlockSpec(memory_space=pltpu.VMEM)
SMEM = pl.BlockSpec(memory_space=pltpu.SMEM)


def call(kernel, name, args, outs, scratch, flops, smem_first=True, after=()):
    read = sum(a.size * a.dtype.itemsize for a in args)
    written = sum(o.size * o.dtype.itemsize for o in outs)
    def body(*refs):
        kernel(*refs[: len(args)], *refs[len(args) + len(after) :])

    return pl.pallas_call(
        body,
        name=name,
        out_shape=outs,
        in_specs=[SMEM if (smem_first and i == 0) else VMEM for i in range(len(args))]
        + [pl.BlockSpec(memory_space=pl.ANY)] * len(after),
        out_specs=[VMEM] * len(outs),
        scratch_shapes=scratch,
        compiler_params=pltpu.CompilerParams(vmem_limit_bytes=VMEM_LIMIT),
        cost_estimate=pl.CostEstimate(
            flops=int(flops * COST), bytes_accessed=int((read + written) * COST), transcendentals=0
        ),
    )(*args, *after)


def shape(dims, kind):
    return jax.ShapeDtypeStruct(dims, kind)


SUMS = shape((8, 8, TOK), jnp.float32)
COLS = pltpu.VMEM((TOK, HD), jnp.float32)
BIAS = pltpu.VMEM((TOK, TOK), jnp.float32)


def squares_call(x, stored, parked):
    return pl.pallas_call(
        squares_kernel,
        name="squares",
        out_shape=SUMS,
        in_specs=[pl.BlockSpec(memory_space=pltpu.HBM)] * 3,
        out_specs=VMEM,
        scratch_shapes=[pltpu.VMEM((3, *x.shape), x.dtype), pltpu.SemaphoreType.DMA((3,))],
        compiler_params=pltpu.CompilerParams(vmem_limit_bytes=WHOLE_VMEM),
    )(x, stored, parked)


def forward_first(micro, lens, x, sums, gain, qgain, other, after=()):
    outs = [shape(x.shape, jnp.bfloat16)] * 2
    return call(
        functools.partial(forward_kernel, micro, 0, True), "forward_first",
        [lens, x, sums, gain, qgain, other], outs, [COLS, BIAS], 3 * 10**9, True, after,
    )


def forward_second(micro, lens, x, sums, gain, qgain, after=()):
    return call(
        functools.partial(forward_kernel, micro, 1, False), "forward_second",
        [lens, x, sums, gain, qgain], [shape(x.shape, jnp.bfloat16), shape((8, HD), jnp.float32)], [COLS, BIAS], 3 * 10**9, True, after,
    )


def backward_call(micro, first, lens, x, dy, sums, gain, qgain, rest, after=()):
    outs = [shape(dy.shape, jnp.float32), SUMS, shape(gain.shape, jnp.float32), shape(gain.shape, jnp.float32)]
    return call(
        functools.partial(backward_kernel, micro, 1 if first else None, first, len(x)),
        "backward_first" if first else "backward_second",
        [lens, *x, dy, sums, gain, qgain] + rest, outs, [COLS, BIAS, COLS], 6 * 10**9, True, after,
    )


def finish_call(first, lens, x, dy, d_unit, sums, project, rest, after=()):
    outs = [shape(dy.shape, jnp.bfloat16)]
    return call(
        functools.partial(finish_kernel, 1 if first else None, first, len(x)),
        "finish_first" if first else "finish_second",
        [lens, *x, dy, d_unit, sums, project] + rest, outs, [COLS, COLS], 10**9, True, after,
    )


def settle_kernel(parts, *refs):
    sources, out, done = refs[:parts], refs[-2], refs[-1]
    copies = []
    at = 0
    for k, source in enumerate(sources):
        rows_n = source.shape[0]
        copies.append(pltpu.make_async_copy(source, out.at[pl.ds(at, rows_n), :], done.at[k]))
        at += rows_n
    for copy in copies:
        copy.start()
    for copy in copies:
        copy.wait()


def settle(parts, after):
    rows_n = sum(part.shape[0] for part in parts)
    return pl.pallas_call(
        functools.partial(settle_kernel, len(parts)),
        name="settle",
        out_shape=shape((rows_n, parts[0].shape[1]), parts[0].dtype),
        in_specs=[VMEM] * len(parts) + [pl.BlockSpec(memory_space=pl.ANY)] * len(after),
        out_specs=pl.BlockSpec(memory_space=pltpu.HBM),
        scratch_shapes=[pltpu.SemaphoreType.DMA((len(parts),))],
        compiler_params=pltpu.CompilerParams(vmem_limit_bytes=SMALL_VMEM),
    )(*parts, *after)


def hold_kernel(*refs):
    pass


def hold(value, after):
    return pl.pallas_call(
        hold_kernel,
        name="hold",
        out_shape=shape(value.shape, value.dtype),
        in_specs=[pl.BlockSpec(memory_space=pl.ANY)] * (1 + len(after)),
        out_specs=pl.BlockSpec(memory_space=pl.ANY),
        input_output_aliases={0: 0},
        compiler_params=pltpu.CompilerParams(vmem_limit_bytes=SMALL_VMEM),
    )(value, *after)


def gathered(sums):
    return lax.all_to_all(sums, "tensor", 0, 0)


def per_device(x_in, grad_in, stash_near, parked_in, fresh, loss_grad, gain, qgain, lengths):
    count = lax.axis_size("section")
    mirrored = [(i, count - 1 - i) for i in range(count)]
    parking = [(i, (count - 2 - i) % count) for i in range(count)]
    onward = [(i, (i + 1) % count) for i in range(count)]
    back = [((i + 1) % count, i) for i in range(count)]
    x, dy, stored, parked = x_in[0], grad_in[0], stash_near[0], parked_in[0]
    fetched = []
    at = 0
    for rows_n in MIRROR_ROWS:
        fetched.append(lax.ppermute(parked[at : at + rows_n], "section", mirrored))
        at += rows_n
    made = {f"m{i}": part for i, part in enumerate(fetched)}

    def after(k):
        return [made[n] for n in AFTER[k]]

    sums = gathered(squares_call(x, stored, parked))
    stored_squares = jnp.sum(sums[:, 2, :], axis=0, keepdims=True)
    stored_squares = lax.ppermute(jnp.broadcast_to(stored_squares, (8, TOK)), "section", mirrored)
    made["tm"] = stored_squares
    d_unit, project, gain_one, qgain_one = backward_call(
        lambda s: s, True, lengths, [stored], dy, sums, gain, qgain, [], after(0)
    )
    project = gathered(project)
    made["a1"] = project
    first_grad = finish_call(
        True, lengths, [stored], dy, d_unit, sums, project, [loss_grad], after(1)
    )[0]
    made["g1"] = first_grad
    d_two = lax.ppermute(first_grad, "section", back)
    made["dx"] = d_two
    first_out, parking_out = forward_first(
        lambda s: 2 * count - 1 - s, lengths, x, sums, gain, qgain, fresh, after(2)
    )
    if HOLD:
        parking_out = hold(parking_out, after(3))
    made["y1"] = first_out
    x_two = lax.ppermute(first_out, "section", onward)
    made["x"] = x_two
    parked_out = [lax.ppermute(parking_out, "section", parking)]
    d_unit, project, gain_two, qgain_two = backward_call(
        lambda s: s + 1, False, lengths, fetched, d_two, stored_squares, gain, qgain,
        [gain_one, qgain_one, x_two], after(4),
    )
    project = gathered(project)
    second_grad = finish_call(
        False, lengths, fetched, d_two, d_unit, stored_squares, project, [], after(5)
    )[0]
    second_out, mark = forward_second(
        lambda s: 2 * count - s, lengths, x_two, project, gain, qgain, after(6)
    )
    parked_out = settle(parked_out, [mark])
    return (
        second_out[None],
        second_grad[None],
        parked_out[None],
        gain_two,
        qgain_two,
    )


def solution(mesh):
    wide = P("section", None, "tensor")
    narrow = P(None, "tensor")
    rows = P("section", "tensor")
    return jax.shard_map(
        per_device,
        mesh=mesh,
        in_specs=(wide, wide, wide, wide, narrow, narrow, rows, rows, P()),
        out_specs=(wide, wide, wide, rows, rows),
        check_vma=False,
    )
```

```python
import functools

import jax
import jax.numpy as jnp
from jax import lax
from jax.experimental import pallas as pl
from jax.experimental.pallas import tpu as pltpu
from jax.sharding import PartitionSpec as P

D = 12288
HD = 128
TOK = 256
HALF = 128
EPSILON = 1e-05
LOG2E = 1.4426950408889634
MASKED = -1e30
VMEM_LIMIT = 20 * 1024 * 1024
SMALL_VMEM = 2 * 1024 * 1024
WHOLE_VMEM = 62 * 1024 * 1024
UNROLL = 6
COST = 1.0
AFTER = ((), (), (), ("m0", "tm", "x"), (), (), ())
MIRROR_ROWS = (256,)
HOLD = True

ROWS_ROWS = (((1,), (1,)), ((), ()))
COLS_ROWS = (((0,), (0,)), ((), ()))
PLAIN = (((1,), (0,)), ((), ()))


def matmul(left, right, dims):
    return lax.dot_general(left, right, dims, preferred_element_type=jnp.float32)


def token_row(per_lane):
    return jnp.sum(per_lane.T, axis=0, keepdims=True)


def token_columns(row):
    return jnp.broadcast_to(row, (HD, TOK)).T


def gathered_row(sums_ref, k):
    return jnp.sum(sums_ref[:, k, :], axis=0, keepdims=True)


def inverse_rms(sum_row):
    return lax.rsqrt(sum_row / D + EPSILON)


def head_columns(h):
    return pl.ds(pl.multiple_of(h * HD, HD), HD)


def over_heads(count, body, init=None):
    def step(i, carry):
        for u in range(UNROLL):
            carry = body(i * UNROLL + u, carry)
        return carry

    return lax.fori_loop(0, count // UNROLL, step, init)


def fill_bias(bias, length):
    key = lax.broadcasted_iota(jnp.int32, (TOK, TOK), 0)
    query = lax.broadcasted_iota(jnp.int32, (TOK, TOK), 1)
    bias[...] = jnp.where((key <= query) & (key < length), 0.0, MASKED)


def attention(hidden, query, bias):
    low = matmul(hidden[:HALF], query, ROWS_ROWS) + bias[:HALF, :]
    high = matmul(hidden[HALF:], query[HALF:], ROWS_ROWS) + bias[HALF:, HALF:]
    top_low = jnp.max(low, axis=0, keepdims=True)
    top_high = jnp.maximum(top_low[:, HALF:], jnp.max(high, axis=0, keepdims=True))
    top = jnp.concatenate([top_low[:, :HALF], top_high], axis=1)
    low = jnp.exp2((low - top) * LOG2E)
    high = jnp.exp2((high - top_high) * LOG2E)
    total_low = jnp.sum(low, axis=0, keepdims=True)
    total_high = total_low[:, HALF:] + jnp.sum(high, axis=0, keepdims=True)
    scale_high = 1.0 / total_high
    scale = jnp.concatenate([1.0 / total_low[:, :HALF], scale_high], axis=1)
    return low * scale, high * scale_high


def over_queries(low, high, right):
    first = matmul(low[:, :HALF], right[:HALF], COLS_ROWS)
    second = matmul(jnp.concatenate([low[:, HALF:], high], axis=0), right, COLS_ROWS)
    return jnp.concatenate([first, second], axis=0)


def squares(ref):
    total = None
    for h in range(ref.shape[1] // HD):
        block = ref[:, h * HD : (h + 1) * HD].astype(jnp.float32)
        total = block * block if total is None else total + block * block
    return token_row(total)


def put_rows(out_ref, rows):
    stacked = jnp.concatenate(rows + [jnp.zeros((8 - len(rows), TOK), jnp.float32)], axis=0)
    out_ref[...] = jnp.broadcast_to(stacked[None], out_ref.shape)


def squares_kernel(x_ref, stored_ref, parked_ref, out_ref, held, arrived):
    refs = (x_ref, stored_ref, parked_ref)
    copies = [pltpu.make_async_copy(r, held.at[k], arrived.at[k]) for k, r in enumerate(refs)]
    for copy in copies:
        copy.start()
    rows = []
    for k, copy in enumerate(copies):
        copy.wait()
        rows.append(squares(held.at[k]))
    put_rows(out_ref, rows)


def forward_kernel(micro, pick, select, len_ref, x_ref, sums_ref, gain_ref, qgain_ref, *rest):
    if select:
        other_ref, y_ref, copy_ref, inv, bias = rest
    else:
        y_ref, mark_ref, inv, bias = rest
        mark_ref[...] = jnp.zeros_like(mark_ref)
    if pick is None:
        row = sums_ref[0:1, :]
    else:
        row = gathered_row(sums_ref, pick)
    inv[...] = token_columns(inverse_rms(row))
    fill_bias(bias, len_ref[micro(lax.axis_index("section"))])
    def body(h, carry):
        cols = head_columns(h)
        x = x_ref[:, cols].astype(jnp.float32)
        normed = x * inv[...] * gain_ref[0:1, cols]
        hidden = normed.astype(jnp.bfloat16)
        query = (normed * (qgain_ref[0:1, cols] * (1.0 / HD))).astype(jnp.bfloat16)
        low, high = attention(hidden, query, bias)
        mixed = over_queries(low.astype(jnp.bfloat16), high.astype(jnp.bfloat16), hidden)
        y = (x + mixed).astype(jnp.bfloat16)
        if select:
            y = jnp.where(lax.axis_index("section") == lax.axis_size("section") - 1, other_ref[:, cols], y)
        y_ref[:, cols] = y
        if select:
            copy_ref[:, cols] = y
        return carry

    over_heads(x_ref.shape[1] // HD, body)


def rows_of(refs, cols):
    return jnp.concatenate([r[:, cols].astype(jnp.float32) for r in refs], axis=0)


def backward_kernel(micro, pick, first, parts, len_ref, *rest):
    x_refs, (dy_ref, sums_ref, gain_ref, qgain_ref), rest = rest[:parts], rest[parts : parts + 4], rest[parts + 4 :]
    if first:
        d_unit_ref, sums_out_ref, gain_out, qgain_out, inv, bias, total = rest
    else:
        gain_in, qgain_in, next_ref, d_unit_ref, sums_out_ref, gain_out, qgain_out, inv, bias, total = rest
    if pick is None:
        row = sums_ref[0:1, :]
    else:
        row = gathered_row(sums_ref, pick)
    inv[...] = token_columns(inverse_rms(row))
    fill_bias(bias, len_ref[micro(lax.axis_index("section"))])
    total[...] = jnp.zeros_like(total)

    def body(h, carry):
        cols = head_columns(h)
        unit = rows_of(x_refs, cols) * inv[...]
        gain = gain_ref[0:1, cols]
        small_qgain = qgain_ref[0:1, cols] * (1.0 / HD)
        normed = unit * gain
        hidden = normed.astype(jnp.bfloat16)
        query = (normed * small_qgain).astype(jnp.bfloat16)
        dy = dy_ref[:, cols]
        low, high = attention(hidden, query, bias)
        d_low = matmul(hidden[:HALF], dy, ROWS_ROWS)
        d_high = matmul(hidden[HALF:], dy[HALF:], ROWS_ROWS)
        mean_low = jnp.sum(low * d_low, axis=0, keepdims=True)
        mean_high = mean_low[:, HALF:] + jnp.sum(high * d_high, axis=0, keepdims=True)
        mean = jnp.concatenate([mean_low[:, :HALF], mean_high], axis=1)
        ds_low = (low * (d_low - mean)).astype(jnp.bfloat16)
        ds_high = (high * (d_high - mean_high)).astype(jnp.bfloat16)
        low = low.astype(jnp.bfloat16)
        high = high.astype(jnp.bfloat16)
        first_keys = matmul(
            jnp.concatenate([ds_low, low], axis=1), jnp.concatenate([query, dy], axis=0), PLAIN
        )
        last_keys = matmul(
            jnp.concatenate([ds_high, high], axis=1),
            jnp.concatenate([query[HALF:], dy[HALF:]], axis=0),
            PLAIN,
        )
        d_query = over_queries(ds_low, ds_high, hidden)
        d_normed = d_query * small_qgain + jnp.concatenate([first_keys, last_keys], axis=0)
        qgain_part = jnp.sum(d_query * normed, axis=0, keepdims=True) * (1.0 / HD)
        along = d_normed * unit
        gain_part = jnp.sum(along, axis=0, keepdims=True)
        if not first:
            qgain_part = qgain_part + qgain_in[0:1, cols]
            gain_part = gain_part + gain_in[0:1, cols]
        qgain_out[0:1, cols] = qgain_part
        gain_out[0:1, cols] = gain_part
        total[...] += along * gain
        d_unit_ref[:, cols] = d_normed * gain
        return carry

    over_heads(dy_ref.shape[1] // HD, body)
    rows = [token_row(total[...])]
    if not first:
        rows.append(squares(next_ref))
    put_rows(sums_out_ref, rows)


def finish_kernel(pick, first, parts, flag_ref, *rest):
    x_refs, (dy_ref, d_unit_ref, sums_ref, project_ref), rest = rest[:parts], rest[parts : parts + 4], rest[parts + 4 :]
    if first:
        other_ref, out_ref, inv, project = rest
    else:
        out_ref, inv, project = rest
    if pick is None:
        row = sums_ref[0:1, :]
    else:
        row = gathered_row(sums_ref, pick)
    inv[...] = token_columns(inverse_rms(row))
    project[...] = token_columns(gathered_row(project_ref, 0) / D)
    for h in range(dy_ref.shape[1] // HD):
        cols = slice(h * HD, (h + 1) * HD)
        unit = rows_of(x_refs, cols) * inv[...]
        dx = dy_ref[:, cols].astype(jnp.float32) + inv[...] * (
            d_unit_ref[:, cols] - unit * project[...]
        )
        dx = dx.astype(jnp.bfloat16)
        if first:
            dx = jnp.where(lax.axis_index("section") == 0, other_ref[:, cols], dx)
        out_ref[:, cols] = dx


VMEM = pl.BlockSpec(memory_space=pltpu.VMEM)
SMEM = pl.BlockSpec(memory_space=pltpu.SMEM)


def call(kernel, name, args, outs, scratch, flops, smem_first=True, after=()):
    read = sum(a.size * a.dtype.itemsize for a in args)
    written = sum(o.size * o.dtype.itemsize for o in outs)
    def body(*refs):
        kernel(*refs[: len(args)], *refs[len(args) + len(after) :])

    return pl.pallas_call(
        body,
        name=name,
        out_shape=outs,
        in_specs=[SMEM if (smem_first and i == 0) else VMEM for i in range(len(args))]
        + [pl.BlockSpec(memory_space=pl.ANY)] * len(after),
        out_specs=[VMEM] * len(outs),
        scratch_shapes=scratch,
        compiler_params=pltpu.CompilerParams(vmem_limit_bytes=VMEM_LIMIT),
        cost_estimate=pl.CostEstimate(
            flops=int(flops * COST), bytes_accessed=int((read + written) * COST), transcendentals=0
        ),
    )(*args, *after)


def shape(dims, kind):
    return jax.ShapeDtypeStruct(dims, kind)


SUMS = shape((8, 8, TOK), jnp.float32)
COLS = pltpu.VMEM((TOK, HD), jnp.float32)
BIAS = pltpu.VMEM((TOK, TOK), jnp.float32)


def squares_call(x, stored, parked):
    return pl.pallas_call(
        squares_kernel,
        name="squares",
        out_shape=SUMS,
        in_specs=[pl.BlockSpec(memory_space=pltpu.HBM)] * 3,
        out_specs=VMEM,
        scratch_shapes=[pltpu.VMEM((3, *x.shape), x.dtype), pltpu.SemaphoreType.DMA((3,))],
        compiler_params=pltpu.CompilerParams(vmem_limit_bytes=WHOLE_VMEM),
    )(x, stored, parked)


def forward_first(micro, lens, x, sums, gain, qgain, other, after=()):
    outs = [shape(x.shape, jnp.bfloat16)] * 2
    return call(
        functools.partial(forward_kernel, micro, 0, True), "forward_first",
        [lens, x, sums, gain, qgain, other], outs, [COLS, BIAS], 3 * 10**9, True, after,
    )


def forward_second(micro, lens, x, sums, gain, qgain, after=()):
    return call(
        functools.partial(forward_kernel, micro, 1, False), "forward_second",
        [lens, x, sums, gain, qgain], [shape(x.shape, jnp.bfloat16), shape((8, HD), jnp.float32)], [COLS, BIAS], 3 * 10**9, True, after,
    )


def backward_call(micro, first, lens, x, dy, sums, gain, qgain, rest, after=()):
    outs = [shape(dy.shape, jnp.float32), SUMS, shape(gain.shape, jnp.float32), shape(gain.shape, jnp.float32)]
    return call(
        functools.partial(backward_kernel, micro, 1 if first else None, first, len(x)),
        "backward_first" if first else "backward_second",
        [lens, *x, dy, sums, gain, qgain] + rest, outs, [COLS, BIAS, COLS], 6 * 10**9, True, after,
    )


def finish_call(first, lens, x, dy, d_unit, sums, project, rest, after=()):
    outs = [shape(dy.shape, jnp.bfloat16)]
    return call(
        functools.partial(finish_kernel, 1 if first else None, first, len(x)),
        "finish_first" if first else "finish_second",
        [lens, *x, dy, d_unit, sums, project] + rest, outs, [COLS, COLS], 10**9, True, after,
    )


def settle_kernel(parts, *refs):
    sources, out, done = refs[:parts], refs[-2], refs[-1]
    copies = []
    at = 0
    for k, source in enumerate(sources):
        rows_n = source.shape[0]
        copies.append(pltpu.make_async_copy(source, out.at[pl.ds(at, rows_n), :], done.at[k]))
        at += rows_n
    for copy in copies:
        copy.start()
    for copy in copies:
        copy.wait()


def settle(parts, after):
    rows_n = sum(part.shape[0] for part in parts)
    return pl.pallas_call(
        functools.partial(settle_kernel, len(parts)),
        name="settle",
        out_shape=shape((rows_n, parts[0].shape[1]), parts[0].dtype),
        in_specs=[VMEM] * len(parts) + [pl.BlockSpec(memory_space=pl.ANY)] * len(after),
        out_specs=pl.BlockSpec(memory_space=pltpu.HBM),
        scratch_shapes=[pltpu.SemaphoreType.DMA((len(parts),))],
        compiler_params=pltpu.CompilerParams(vmem_limit_bytes=SMALL_VMEM),
    )(*parts, *after)


def hold_kernel(*refs):
    pass


def hold(value, after):
    return pl.pallas_call(
        hold_kernel,
        name="hold",
        out_shape=shape(value.shape, value.dtype),
        in_specs=[pl.BlockSpec(memory_space=pl.ANY)] * (1 + len(after)),
        out_specs=pl.BlockSpec(memory_space=pl.ANY),
        input_output_aliases={0: 0},
        compiler_params=pltpu.CompilerParams(vmem_limit_bytes=SMALL_VMEM),
    )(value, *after)


def gathered(sums):
    return lax.all_to_all(sums, "tensor", 0, 0)


def per_device(x_in, grad_in, stash_near, parked_in, fresh, loss_grad, gain, qgain, lengths):
    count = lax.axis_size("section")
    mirrored = [(i, count - 1 - i) for i in range(count)]
    parking = [(i, (count - 2 - i) % count) for i in range(count)]
    onward = [(i, (i + 1) % count) for i in range(count)]
    back = [((i + 1) % count, i) for i in range(count)]
    x, dy, stored, parked = x_in[0], grad_in[0], stash_near[0], parked_in[0]
    fetched = []
    at = 0
    for rows_n in MIRROR_ROWS:
        fetched.append(lax.ppermute(parked[at : at + rows_n], "section", mirrored))
        at += rows_n
    made = {f"m{i}": part for i, part in enumerate(fetched)}

    def after(k):
        return [made[n] for n in AFTER[k]]

    sums = gathered(squares_call(x, stored, parked))
    stored_squares = jnp.sum(sums[:, 2, :], axis=0, keepdims=True)
    stored_squares = lax.ppermute(jnp.broadcast_to(stored_squares, (8, TOK)), "section", mirrored)
    made["tm"] = stored_squares
    d_unit, project, gain_one, qgain_one = backward_call(
        lambda s: s, True, lengths, [stored], dy, sums, gain, qgain, [], after(0)
    )
    project = gathered(project)
    made["a1"] = project
    first_grad = finish_call(
        True, lengths, [stored], dy, d_unit, sums, project, [loss_grad], after(1)
    )[0]
    made["g1"] = first_grad
    d_two = lax.ppermute(first_grad, "section", back)
    made["dx"] = d_two
    first_out, parking_out = forward_first(
        lambda s: 2 * count - 1 - s, lengths, x, sums, gain, qgain, fresh, after(2)
    )
    made["y1"] = first_out
    x_two = lax.ppermute(first_out, "section", onward)
    made["x"] = x_two
    if HOLD:
        parking_out = hold(parking_out, after(3))
    parked_out = [lax.ppermute(parking_out, "section", parking)]
    d_unit, project, gain_two, qgain_two = backward_call(
        lambda s: s + 1, False, lengths, fetched, d_two, stored_squares, gain, qgain,
        [gain_one, qgain_one, x_two], after(4),
    )
    project = gathered(project)
    second_grad = finish_call(
        False, lengths, fetched, d_two, d_unit, stored_squares, project, [], after(5)
    )[0]
    second_out, mark = forward_second(
        lambda s: 2 * count - s, lengths, x_two, project, gain, qgain, after(6)
    )
    parked_out = settle(parked_out, [mark])
    return (
        second_out[None],
        second_grad[None],
        parked_out[None],
        gain_two,
        qgain_two,
    )


def solution(mesh):
    wide = P("section", None, "tensor")
    narrow = P(None, "tensor")
    rows = P("section", "tensor")
    return jax.shard_map(
        per_device,
        mesh=mesh,
        in_specs=(wide, wide, wide, wide, narrow, narrow, rows, rows, P()),
        out_specs=(wide, wide, wide, rows, rows),
        check_vma=False,
    )
```
